512 devices in a mesh: ka: 32 (over z_lo, y), grid: 16 (over z_hi, x, core).
Axes of the slice: x: 4, y: 8, z: 8 (z_hi: 2, z_lo: 4; z = z_hi * 4 + z_lo), core: 2. Of those that a mesh axis runs over, the one named last changes fastest.
Arguments:
- wavefunctions: bfloat16 [32, 512, 2, 2048], P('ka', 'grid'), may hold values from -3 to 3
- projectors: bfloat16 [512, 256], replicated, may hold values from -0.25 to 0.25
- support: int32 [32, 16], replicated, may hold values 0 or 1
- proj_counts: int32 [32], replicated, may hold values from 1 to 8
- aug_matrices: float32 [32, 8, 8], replicated, may hold values from -6 to 6
- atom_sites: float32 [32, 3], replicated, may hold values from 0 to 1
- b_vectors: float32 [2, 3], replicated, may hold values from -0.5 to 0.5
- partner: int32 [32, 2], P('ka'), may hold values from 0 to 31, as said below
- lattice_shift: int32 [32, 2, 3], P('ka'), may hold values from -1 to 1
Outputs:
- correlations: bfloat16 [32, 2, 2, 2048, 2048], P('ka', None, None, 'grid')
The draws below stay inside these ranges and needn't reach their ends.
Inputs may be any that keep to these rules, and one draw needn't show every extreme that they name: For each of the two b-vectors, partner[k, v] - k modulo 32 is the same for every k; the two b-vectors' differences are independent of each other.
All inputs are finite; a program needn't handle non-finite values.
Results may differ from the reference program's by a relative error of at most 0.0057.
Values may be sent and summed in bfloat16 or wider, within the bound.
No kernel may reach another device: no remote copies, remote signals or barrier semaphores. Data moves between devices by JAX's collectives and lax.ppermute only.
A program may use at most 64 MiB of HBM per device.

```python
import math
import jax
import jax.numpy as jnp
from jax import lax

BANDS = 2048
ATOMS = 32
PROJ_ATOM = 8
SIDE = 16
DEPTH = 96
KPTS = 32
ROWS = 512
SLABS = 16
NPROJ = 256


def draw_partner(key, part):
    key = jax.random.fold_in(key, 11)
    first_key, second_key = jax.random.split(key)
    first_distance = jax.random.randint(first_key, (), 1, KPTS, dtype=jnp.int32)
    second_distance = jax.random.randint(second_key, (), 1, KPTS, dtype=jnp.int32)
    point_ids = jnp.arange(KPTS, dtype=jnp.int32)
    return jnp.stack([(point_ids + first_distance) % KPTS, (point_ids + second_distance) % KPTS], axis=1).astype(jnp.int32)


def set_ends(entries, stream_key, smallest, largest):
    longest = entries.shape.index(max(entries.shape))
    spots = []
    for shift in (0, 1):
        where = [jax.random.randint(jax.random.fold_in(stream_key, axis), (), 0, length) for axis, length in enumerate(entries.shape)]
        where[longest] = (where[longest] + shift) % entries.shape[longest]
        spots.append(tuple(where))
    return entries.at[spots[0]].set(smallest).at[spots[1]].set(largest)


def steps_of(key, shape, shards, least, top_value):
    factor_of, own = 1.0, jax.random.fold_in(key, 6)
    for dim, parts in shards:
        draws = jnp.exp(jax.random.uniform(jax.random.fold_in(own, dim), (parts,), jnp.float32, least / len(shards), top_value / len(shards)))
        factor_of = factor_of * jnp.repeat(draws, shape[dim] // parts).reshape([-1 if axis == dim else 1 for axis in range(len(shape))])
    return factor_of


def centred(stream_key, shape, scale, limit, pieces=(), kind=jnp.bfloat16):
    gain = steps_of(stream_key, shape, pieces, -0.22, 0.18) if pieces else 1.0
    entries = jax.random.normal(stream_key, shape, jnp.float32) * scale * gain
    return jnp.minimum(jnp.maximum(entries, -limit), limit).astype(kind)


def setup_inputs(seed: int = 0) -> dict:
    streams_of = jax.random.split(jax.random.key(seed), 10)
    return {
        "wavefunctions": centred(streams_of[0], (KPTS, ROWS, 2, BANDS), (ROWS ** -0.25), 3.0, ((0, 32), (1, 16))),
        "projectors": centred(streams_of[1], (ROWS, NPROJ), ROWS ** -0.5, 0.25),
        "support": set_ends((jax.random.randint(streams_of[2], (ATOMS, SLABS), 0, 4) < 3).astype(jnp.int32), jax.random.fold_in(streams_of[2], 1), 0, 1),
        "proj_counts": set_ends(jax.random.randint(streams_of[3], (ATOMS,), 1, PROJ_ATOM + 1), jax.random.fold_in(streams_of[3], 1), 1, PROJ_ATOM).astype(jnp.int32),
        "aug_matrices": centred(streams_of[4], (ATOMS, PROJ_ATOM, PROJ_ATOM), 1.0, 6.0, (), jnp.float32),
        "atom_sites": jnp.clip(jax.random.uniform(streams_of[5], (ATOMS, 3), jnp.float32, 0.0, 1.0), 0.0, 1.0),
        "b_vectors": jnp.clip(jax.random.uniform(streams_of[6], (2, 3), jnp.float32, -0.5, 0.5), -0.5, 0.5),
        "partner": draw_partner(jax.random.fold_in(streams_of[9], 71), 0),
        "lattice_shift": set_ends(jax.random.randint(streams_of[8], (KPTS, 2, 3), -1, 2), jax.random.fold_in(streams_of[8], 1), -1, 1).astype(jnp.int32),
    }


TWO_PI = 2.0 * math.pi


def row_angles(wave_vector, row_start, row_count):
    row_ids = row_start + jnp.arange(row_count, dtype=jnp.int32)
    along_a = (row_ids % SIDE).astype(jnp.float32) / SIDE
    along_b = ((row_ids // SIDE) % SIDE).astype(jnp.float32) / SIDE
    along_c = (row_ids // (SIDE * SIDE)).astype(jnp.float32) / DEPTH
    return TWO_PI * (wave_vector[0] * along_a + wave_vector[1] * along_b + wave_vector[2] * along_c)


def phased(partner_rows, angles):
    cosine = jnp.cos(angles)[:, None]
    sine = jnp.sin(angles)[:, None]
    real_part = partner_rows[:, 0].astype(jnp.float32)
    imag_part = partner_rows[:, 1].astype(jnp.float32)
    return jnp.stack([cosine * real_part + sine * imag_part, cosine * imag_part - sine * real_part], axis=1).astype(jnp.bfloat16)


def masked_beta(projectors, support, proj_counts, per_atom):
    atom_count = support.shape[0]
    slab_count = support.shape[1]
    row_dev = projectors.shape[0] // slab_count
    live = (jnp.arange(per_atom, dtype=jnp.int32)[None, :] < proj_counts[:, None]).astype(jnp.int32)
    keep = jnp.transpose(support)[:, None, :, None] * live[None, None, :, :]
    keep = jnp.broadcast_to(keep, (slab_count, row_dev, atom_count, per_atom)).reshape(projectors.shape)
    return projectors * keep.astype(projectors.dtype)


def project(weights, rows_block):
    width = rows_block.shape[2]
    flat = rows_block.reshape(rows_block.shape[0], 2 * width)
    result = lax.dot_general(weights, flat, (((0,), (0,)), ((), ())), preferred_element_type=jnp.float32)
    return result.reshape(weights.shape[1], 2, width)


def augment(proj_other, aug_matrices, atom_sites, wave_vector):
    atom_count = aug_matrices.shape[0]
    per_atom = aug_matrices.shape[1]
    width = proj_other.shape[2]
    phase = TWO_PI * (wave_vector[0] * atom_sites[:, 0] + wave_vector[1] * atom_sites[:, 1] + wave_vector[2] * atom_sites[:, 2])
    cos_part = aug_matrices * jnp.cos(phase)[:, None, None]
    sin_part = -aug_matrices * jnp.sin(phase)[:, None, None]
    real_proj = proj_other[:, 0].astype(jnp.float32).reshape(atom_count, per_atom, width)
    imag_proj = proj_other[:, 1].astype(jnp.float32).reshape(atom_count, per_atom, width)
    highest = lax.Precision.HIGHEST
    real_w = jnp.einsum("aij,ajn->ain", cos_part, real_proj, precision=highest) - jnp.einsum("aij,ajn->ain", sin_part, imag_proj, precision=highest)
    imag_w = jnp.einsum("aij,ajn->ain", cos_part, imag_proj, precision=highest) + jnp.einsum("aij,ajn->ain", sin_part, real_proj, precision=highest)
    return jnp.stack([real_w.reshape(atom_count * per_atom, width), imag_w.reshape(atom_count * per_atom, width)], axis=1).astype(jnp.bfloat16)


def correlation(left, right):
    stacked_left = jnp.concatenate([left[:, 0], left[:, 1]], axis=0)
    real_right = right[:, 0]
    imag_right = right[:, 1]
    stacked_right = jnp.concatenate([jnp.concatenate([real_right, imag_right], axis=1), jnp.concatenate([imag_right, -real_right], axis=1)], axis=0)
    return lax.dot_general(stacked_left, stacked_right, (((0,), (0,)), ((), ())), preferred_element_type=jnp.float32)


def two_parts(total, width):
    return jnp.stack([total[:, :width], total[:, width:]])


def reference(wavefunctions, projectors, support, proj_counts, aug_matrices, atom_sites, b_vectors, partner, lattice_shift):
    weights = masked_beta(projectors, support, proj_counts, PROJ_ATOM)

    def one_point(kpoint):
        own_waves = wavefunctions[kpoint]
        proj_own = project(weights, own_waves).astype(jnp.bfloat16)
        results = []
        for vector_id in range(2):
            other_waves = wavefunctions[partner[kpoint, vector_id]]
            wave_vector = b_vectors[vector_id] + lattice_shift[kpoint, vector_id].astype(jnp.float32)
            shifted = phased(other_waves, row_angles(wave_vector, 0, ROWS))
            proj_other = project(weights, other_waves).astype(jnp.bfloat16)
            aug_weights = augment(proj_other, aug_matrices, atom_sites, wave_vector)
            total = correlation(own_waves, shifted) + correlation(proj_own, aug_weights)
            results.append(two_parts(total, BANDS))
        return jnp.stack(results).astype(jnp.bfloat16)

    return lax.map(one_point, jnp.arange(KPTS, dtype=jnp.int32))
```

```python
import functools
import math

import jax
import jax.numpy as jnp
from jax import lax
from jax.experimental import pallas as pl
from jax.experimental.pallas import tpu as pltpu
from jax.sharding import PartitionSpec as P

SIDE = 16
DEPTH = 96
TWO_PI = 2.0 * math.pi

Z_LO, Y, Z_HI, X, CORE = 4, 8, 2, 4, 2
Z = Z_LO * Z_HI
POINTS = Z_LO * Y
AXES = ("ka", "grid")
SLABS = 16
SLAB_ROWS = 32
PER_ATOM = 8
HIGHEST = lax.Precision.HIGHEST


def flat_id(x, y, z, core):
    return (((z % Z_LO) * Y + y) * Z_HI + z // Z_LO) * (X * CORE) + x * CORE + core


def route(source_of):
    pairs = []
    for x in range(X):
        for y in range(Y):
            for z in range(Z):
                for core in range(CORE):
                    sx, sy, sz, sc = source_of(x, y, z, core)
                    pairs.append(
                        (flat_id(sx % X, sy % Y, sz % Z, sc), flat_id(x, y, z, core))
                    )
    return pairs


def moved(block, source_of):
    return lax.ppermute(block, AXES, route(source_of))


def from_other_core(block):
    return moved(block, lambda x, y, z, core: (x, y, z, 1 - core))


def from_x(block, offset):
    return moved(block, lambda x, y, z, core: (x + offset, y, z, core))


def along_y(lane, steps):
    if steps == 0:
        return lane
    return moved(
        lane,
        lambda x, y, z, core: (x, y + steps, z + (y + steps) // Y, core),
    )


def along_z(lane, steps):
    ahead = lane
    if steps:
        ahead = moved(lane, lambda x, y, z, core: (x, y, z + steps, core))
    return ahead, moved(lane, lambda x, y, z, core: (x, y, z + steps + Z_LO, core))


def near_pieces(held):
    ahead, behind = held
    left_ahead, right_behind = from_x(ahead, -1), from_x(behind, 1)
    return left_ahead, from_x(behind, -1), from_x(ahead, 1), right_behind


def far_pieces(near):
    return from_x(near[0], -1), from_x(near[3], 1)


def dot00(left, right, precision=None):
    return lax.dot_general(
        left,
        right,
        (((0,), (0,)), ((), ())),
        precision=precision,
        preferred_element_type=jnp.float32,
    )


def left_kernel(
    slot_ref,
    b_ref,
    shift_ref,
    own_ref,
    other_ref,
    proj_ref,
    support_ref,
    counts_ref,
    aug_ref,
    sites_ref,
    out_ref,
    real_ref,
    imag_ref,
    masked_ref,
):
    atoms = support_ref.shape[0]
    nproj = proj_ref.shape[1]
    rows = proj_ref.shape[0]
    width = own_ref.shape[1]
    f32 = jnp.float32

    atom_of = lax.broadcasted_iota(jnp.int32, (atoms, nproj), 1) // PER_ATOM
    spread = (atom_of == lax.broadcasted_iota(jnp.int32, (atoms, nproj), 0)).astype(f32)
    reach = dot00(support_ref[...].astype(f32), spread)
    counts = jnp.broadcast_to(counts_ref[...].astype(f32), (8, atoms))
    counts = jnp.dot(counts, spread, preferred_element_type=f32)[0:1]
    slot_id = (lax.broadcasted_iota(jnp.int32, (1, nproj), 1) % PER_ATOM).astype(f32)
    keep = reach * (slot_id < counts - 0.5).astype(f32)
    for s in range(SLABS):
        at = pl.ds(s * SLAB_ROWS, SLAB_ROWS)
        masked_ref[at, :] = (proj_ref[at, :].astype(f32) * keep[s : s + 1, :]).astype(
            jnp.bfloat16
        )
        first = pl.ds(s * 2 * SLAB_ROWS, SLAB_ROWS)
        second = pl.ds(s * 2 * SLAB_ROWS + SLAB_ROWS, SLAB_ROWS)
        real_ref[at, 0:width] = own_ref[first, :]
        real_ref[at, width : 2 * width] = other_ref[first, :]
        imag_ref[at, 0:width] = own_ref[second, :]
        imag_ref[at, width : 2 * width] = other_ref[second, :]

    masked = masked_ref[...]
    proj_real = dot00(masked, real_ref[...]).astype(jnp.bfloat16).astype(f32)
    proj_imag = dot00(masked, imag_ref[...]).astype(jnp.bfloat16).astype(f32)

    pick = (
        lax.broadcasted_iota(jnp.int32, (PER_ATOM, nproj), 1) % PER_ATOM
        == lax.broadcasted_iota(jnp.int32, (PER_ATOM, nproj), 0)
    ).astype(f32)
    tiled = jnp.dot(aug_ref[...], pick, precision=HIGHEST, preferred_element_type=f32)
    same_atom = (
        lax.broadcasted_iota(jnp.int32, (nproj, nproj), 0) // PER_ATOM
        == lax.broadcasted_iota(jnp.int32, (nproj, nproj), 1) // PER_ATOM
    )
    aug = jnp.where(same_atom, tiled, 0.0)
    aug_real = jnp.dot(aug, proj_real, precision=HIGHEST, preferred_element_type=f32)
    aug_imag = jnp.dot(aug, proj_imag, precision=HIGHEST, preferred_element_type=f32)

    sites = jnp.dot(sites_ref[...], spread, precision=HIGHEST, preferred_element_type=f32)
    chunks = rows // 128
    lanes = lax.broadcasted_iota(jnp.int32, (8, 128), 1)
    block = lax.broadcasted_iota(jnp.int32, (8, 128), 0)
    row_ids = block * 128 + lanes
    along_a = (row_ids % SIDE).astype(f32) / SIDE
    along_b = (row_ids // SIDE % SIDE).astype(f32) / SIDE
    along_c = (row_ids // (SIDE * SIDE)).astype(f32) / DEPTH

    for v in range(2):
        q = [b_ref[v, axis] + shift_ref[v, axis].astype(f32) for axis in range(3)]
        theta = TWO_PI * (q[0] * along_a + q[1] * along_b + q[2] * along_c)
        phi = TWO_PI * (q[0] * sites[0:1] + q[1] * sites[1:2] + q[2] * sites[2:3])
        angle = theta
        for part in range(nproj // 128):
            piece = phi[0:1, part * 128 : (part + 1) * 128]
            angle = jnp.where(block == chunks + part, piece, angle)
        cosine = jnp.transpose(jnp.cos(angle))
        sine = jnp.transpose(jnp.sin(angle))
        weights = []
        for part in range(nproj // 128):
            at = slice(part * 128, (part + 1) * 128)
            cos_p = cosine[:, chunks + part : chunks + part + 1]
            sin_p = sine[:, chunks + part : chunks + part + 1]
            weights.append(
                (
                    cos_p * aug_real[at] - sin_p * aug_imag[at],
                    cos_p * aug_imag[at] + sin_p * aug_real[at],
                )
            )
        weight_real = jnp.concatenate([w[0] for w in weights], axis=0)
        weight_imag = jnp.concatenate([w[1] for w in weights], axis=0)

        def spread_rows(weight):
            high = weight.astype(jnp.bfloat16)
            low = (weight - high.astype(f32)).astype(jnp.bfloat16)
            return jnp.dot(masked, high, preferred_element_type=f32) + jnp.dot(
                masked, low, preferred_element_type=f32
            )

        added_real = spread_rows(weight_real)
        added_imag = spread_rows(weight_imag)
        per_chunk = 128 // SLAB_ROWS
        for s in range(SLABS):
            chunk, inside = s // per_chunk, s % per_chunk * SLAB_ROWS
            at = slice(s * SLAB_ROWS, (s + 1) * SLAB_ROWS)
            cos_r = cosine[inside : inside + SLAB_ROWS, chunk : chunk + 1]
            sin_r = sine[inside : inside + SLAB_ROWS, chunk : chunk + 1]
            wave_real = real_ref[at, :].astype(f32)
            wave_imag = imag_ref[at, :].astype(f32)
            left_real = cos_r * wave_real - sin_r * wave_imag + added_real[at]
            left_imag = cos_r * wave_imag + sin_r * wave_real + added_imag[at]
            left_real = left_real.astype(jnp.bfloat16)
            left_imag = left_imag.astype(jnp.bfloat16)
            slot = slot_ref[v, s]
            top, low = pl.ds(0, SLAB_ROWS), pl.ds(SLAB_ROWS, SLAB_ROWS)
            for side in range(2):
                real_half = left_real[:, side * width : (side + 1) * width]
                imag_half = left_imag[:, side * width : (side + 1) * width]
                base = side * 2 * width
                out_ref[v, slot, top, base : base + width] = real_half
                out_ref[v, slot, low, base : base + width] = imag_half
                out_ref[v, slot, top, base + width : base + 2 * width] = -imag_half
                out_ref[v, slot, low, base + width : base + 2 * width] = real_half


def left_operators(slots, b_vectors, shift, own, other, projectors, support, counts, aug, sites):
    rows, nproj = projectors.shape
    width = own.shape[1]
    smem = pl.BlockSpec(memory_space=pltpu.SMEM)
    vmem = pl.BlockSpec(memory_space=pltpu.VMEM)
    return pl.pallas_call(
        left_kernel,
        out_shape=jax.ShapeDtypeStruct((2, SLABS, 2 * SLAB_ROWS, 4 * width), jnp.bfloat16),
        in_specs=[smem] * 3 + [vmem] * 7,
        out_specs=vmem,
        scratch_shapes=[
            pltpu.VMEM((rows, 2 * width), jnp.bfloat16),
            pltpu.VMEM((rows, 2 * width), jnp.bfloat16),
            pltpu.VMEM((rows, nproj), jnp.bfloat16),
        ],
        compiler_params=pltpu.CompilerParams(vmem_limit_bytes=32 * 1024 * 1024),
        cost_estimate=pl.CostEstimate(
            flops=2_000_000_000, bytes_accessed=4 * 1024 * 1024, transcendentals=4096
        ),
        name="left_operators",
    )(slots, b_vectors, shift, own, other, projectors, support, counts, aug, sites)


def product_kernel(left_ref, *refs):
    pieces, (mine_ref, theirs_ref) = refs[:-2], refs[-2:]
    half = mine_ref.shape[0]
    right = jnp.concatenate([piece[...] for piece in pieces], axis=0)
    for side, out_ref in enumerate((mine_ref, theirs_ref)):
        left = left_ref[:, side * half : (side + 1) * half]
        out_ref[...] = dot00(left, right).astype(jnp.bfloat16)


def product(left, pieces):
    depth, wide = left.shape
    columns = pieces[0].shape[1]
    tile = 256
    half = wide // 2
    return pl.pallas_call(
        product_kernel,
        grid=(columns // tile,),
        out_shape=[jax.ShapeDtypeStruct((half, columns), jnp.bfloat16)] * 2,
        in_specs=[pl.BlockSpec((depth, wide), lambda i: (0, 0))]
        + [pl.BlockSpec((p.shape[0], tile), lambda i: (0, i)) for p in pieces],
        out_specs=[pl.BlockSpec((half, tile), lambda i: (0, i))] * 2,
        compiler_params=pltpu.CompilerParams(vmem_limit_bytes=32 * 1024 * 1024),
        cost_estimate=pl.CostEstimate(
            flops=2 * depth * wide * columns,
            bytes_accessed=5 * 1024 * 1024,
            transcendentals=0,
        ),
        name="product",
    )(left, *pieces)


def body(
    wavefunctions,
    projectors,
    support,
    proj_counts,
    aug_matrices,
    atom_sites,
    b_vectors,
    partner,
    lattice_shift,
):
    waves = wavefunctions[0]
    row_count, _, bands = waves.shape
    half_bands = bands // CORE
    point, member = lax.axis_index("ka"), lax.axis_index("grid")
    core, x, z_hi = member % CORE, member // CORE % X, member // (CORE * X)
    y, z_lo = point % Y, point // Y
    z = z_hi * Z_LO + z_lo
    distances = [(partner[0, v] - point) % POINTS for v in range(2)]

    slab = jnp.transpose(waves, (1, 0, 2)).reshape(2 * row_count, bands)
    low, high = slab[:, :half_bands], slab[:, half_bands:]
    kept = jnp.where(core == 0, low, high)
    given = jnp.where(core == 0, high, low)
    lane = jnp.concatenate([kept, from_other_core(given)], axis=0)

    steps_y = [d % Y for d in distances]
    steps_z = [d // Y for d in distances]

    def second_stage(y_second, z_first, lane, moved_first):
        return along_y(lane, y_second), along_z(moved_first, z_first)

    def third_stage(z_second, moved_second, held_first, slab):
        held_second = along_z(moved_second, z_second)
        near_first = near_pieces(held_first)
        own = lax.all_to_all(slab, "grid", split_axis=1, concat_axis=0, tiled=True)
        return held_second, near_first, own

    moved_first = lax.switch(
        steps_y[0], [functools.partial(along_y, steps=s) for s in range(Y)], lane
    )
    moved_second, held_first = lax.switch(
        steps_y[1] * Z_LO + steps_z[0],
        [
            functools.partial(second_stage, y_second, z_first)
            for y_second in range(Y)
            for z_first in range(Z_LO)
        ],
        lane,
        moved_first,
    )
    held_second, near_first, own = lax.switch(
        steps_z[1],
        [functools.partial(third_stage, s) for s in range(Z_LO)],
        moved_second,
        held_first,
        slab,
    )
    other = from_other_core(own)
    slab_ids = jnp.arange(SLABS, dtype=jnp.int32)
    places = []
    for v in range(2):
        ahead_hi = (z + steps_z[v] + (y + steps_y[v]) // Y) % Z // Z_LO
        is_behind = (slab_ids // (CORE * X) != ahead_hi).astype(jnp.int32)
        step = (slab_ids // CORE % X - x) % X
        piece = jnp.where(step == 3, 1, jnp.where(step == 0, 0, step + 1))
        is_other = (slab_ids % CORE != core).astype(jnp.int32)
        places.append(piece * 4 + is_behind * 2 + is_other)
    slots = jnp.stack(places).astype(jnp.int32)
    left = left_operators(
        slots,
        b_vectors,
        lattice_shift[0],
        own,
        other,
        projectors,
        support,
        proj_counts.reshape(1, -1),
        jnp.transpose(aug_matrices, (0, 2, 1)).reshape(-1, PER_ATOM),
        jnp.transpose(atom_sites),
    )
    left = left.reshape(2, left.shape[1] * left.shape[2], left.shape[3])

    far_first = far_pieces(near_first)
    near_second = near_pieces(held_second)
    mine_first, theirs_first = product(left[0], held_first + near_first + far_first)
    got_first = from_other_core(theirs_first)
    far_second = far_pieces(near_second)
    mine_second, theirs_second = product(left[1], held_second + near_second + far_second)
    got_second = from_other_core(theirs_second)

    def joined(mine, got):
        return jnp.concatenate(
            [jnp.where(core == 0, mine, got), jnp.where(core == 0, got, mine)], axis=1
        )

    final = jnp.stack([joined(mine_first, got_first), joined(mine_second, got_second)])
    return final.reshape(1, 2, 2, bands // SLABS, bands)


def solution(mesh):
    in_specs = (
        P("ka", "grid", None, None),
        P(),
        P(),
        P(),
        P(),
        P(),
        P(),
        P("ka", None),
        P("ka", None, None),
    )
    out_specs = P("ka", None, None, "grid", None)
    return jax.shard_map(body, mesh=mesh, in_specs=in_specs, out_specs=out_specs, check_vma=False)
```

```python
import functools
import math

import jax
import jax.numpy as jnp
from jax import lax
from jax.experimental import pallas as pl
from jax.experimental.pallas import tpu as pltpu
from jax.sharding import PartitionSpec as P

SIDE = 16
DEPTH = 96
TWO_PI = 2.0 * math.pi

Z_LO, Y, Z_HI, X, CORE = 4, 8, 2, 4, 2
Z = Z_LO * Z_HI
POINTS = Z_LO * Y
AXES = ("ka", "grid")
SLABS = 16
SLAB_ROWS = 32
PER_ATOM = 8
HIGHEST = lax.Precision.HIGHEST


def flat_id(x, y, z, core):
    return (((z % Z_LO) * Y + y) * Z_HI + z // Z_LO) * (X * CORE) + x * CORE + core


def route(source_of):
    pairs = []
    for x in range(X):
        for y in range(Y):
            for z in range(Z):
                for core in range(CORE):
                    source = source_of(x, y, z, core)
                    if source is None:
                        continue
                    sx, sy, sz, sc = source
                    pairs.append(
                        (flat_id(sx % X, sy % Y, sz % Z, sc), flat_id(x, y, z, core))
                    )
    return pairs


def moved(block, source_of):
    return lax.ppermute(block, AXES, route(source_of))


def from_other_core(block):
    return moved(block, lambda x, y, z, core: (x, y, z, 1 - core))


def from_x(block, offset):
    return moved(block, lambda x, y, z, core: (x + offset, y, z, core))


def z_offset(distance, core, y):
    part = (distance // Y + 2 + (y + distance % Y) // Y) % Z_LO
    other_way = (part == 2) * core * (distance % Y != 0)
    return part - Z_LO * (part == 3) - Z_LO * other_way


class Place:
    def __init__(self, partner):
        point, member = lax.axis_index("ka"), lax.axis_index("grid")
        self.core = member & (CORE - 1)
        self.x = (member >> 1) & (X - 1)
        self.z_hi = member >> 3
        self.y = point & (Y - 1)
        self.z = self.z_hi * Z_LO + (point >> 3)
        distances = [(partner[0, v] - point) & (POINTS - 1) for v in range(2)]
        along = [d & (Y - 1) for d in distances]
        hops = [jnp.minimum(d, Y - d) for d in along]
        swapped = hops[0] > hops[1]
        self.swap = jnp.where(swapped, 1, 0)
        self.distances = [
            jnp.where(swapped, distances[1 - v], distances[v]) for v in range(2)
        ]

    def first_hi(self, v):
        distance = self.distances[v]
        along = distance & (Y - 1)
        part = ((distance >> 3) + 2 + ((self.y + along) >> 3)) & (Z_LO - 1)
        other_way = (part == 2) & (self.core == 1) & (along != 0)
        back = jnp.where((part == 3) | other_way, Z_LO, 0)
        return ((self.z - 2 + part - back) & (Z - 1)) >> 2


def from_other_half(block):
    return moved(
        block,
        lambda x, y, z, core: None if core == z // Z_LO else (x, y, z + Z_LO, 1 - core),
    )


def toward_partner(lane, distance):
    def source(x, y, z, core):
        return x, (y + distance) % Y, z + z_offset(distance, core, y), core

    if all(source(0, y, 0, c) == (0, y, 0, c) for y in range(Y) for c in range(CORE)):
        return lane
    return moved(lane, source)


def both_halves(lane):
    behind = moved(lane, lambda x, y, z, core: (x, y, z - 2, core))
    ahead = moved(lane, lambda x, y, z, core: (x, y, z + 2, core))
    return behind, ahead


def dot00(left, right, precision=None):
    return lax.dot_general(
        left,
        right,
        (((0,), (0,)), ((), ())),
        precision=precision,
        preferred_element_type=jnp.float32,
    )


def left_kernel(
    partner_ref,
    b_ref,
    shift_ref,
    own_ref,
    other_ref,
    proj_ref,
    support_ref,
    counts_ref,
    aug_ref,
    sites_ref,
    out_ref,
    real_ref,
    imag_ref,
    masked_ref,
    both_ref,
):
    atoms = support_ref.shape[1]
    nproj = proj_ref.shape[1]
    rows = proj_ref.shape[0]
    width = own_ref.shape[2] // 2
    place = Place(partner_ref)
    core = place.core
    f32 = jnp.float32

    atom_of = lax.broadcasted_iota(jnp.int32, (atoms, nproj), 1) // PER_ATOM
    spread = (atom_of == lax.broadcasted_iota(jnp.int32, (atoms, nproj), 0)).astype(f32)
    reach = jnp.dot(support_ref[...].astype(f32), spread, preferred_element_type=f32)
    counts = jnp.broadcast_to(counts_ref[...].astype(f32), (8, atoms))
    counts = jnp.dot(counts, spread, preferred_element_type=f32)[0:1]
    slot_id = (lax.broadcasted_iota(jnp.int32, (1, nproj), 1) % PER_ATOM).astype(f32)
    keep = reach * (slot_id < counts - 0.5).astype(f32)
    both_ref[core] = own_ref[...]
    both_ref[1 - core] = other_ref[...]
    for s in range(SLABS):
        at = pl.ds(s * SLAB_ROWS, SLAB_ROWS)
        masked_ref[at, :] = (proj_ref[at, :].astype(f32) * keep[s : s + 1, :]).astype(
            jnp.bfloat16
        )
        slab_hi, slab_x, slab_core = s // (CORE * X), s // CORE % X, s % CORE
        slab = CORE * ((place.x - slab_x) & (X - 1)) + (slab_core ^ place.z_hi)
        for side in range(2):
            lanes = pl.ds(pl.multiple_of((core ^ side) * width, width), width)
            to = pl.ds(side * width, width)
            real_ref[at, to] = both_ref[slab_hi, slab, pl.ds(0, SLAB_ROWS), lanes]
            imag_ref[at, to] = both_ref[slab_hi, slab, pl.ds(SLAB_ROWS, SLAB_ROWS), lanes]

    masked = masked_ref[...]
    proj_real = dot00(masked, real_ref[...]).astype(jnp.bfloat16).astype(f32)
    proj_imag = dot00(masked, imag_ref[...]).astype(jnp.bfloat16).astype(f32)

    by_pair = jnp.dot(aug_ref[...], spread, precision=HIGHEST, preferred_element_type=f32)
    column = lax.broadcasted_iota(jnp.int32, (PER_ATOM, nproj), 1) % PER_ATOM
    pick = column == lax.broadcasted_iota(jnp.int32, (PER_ATOM, nproj), 0)
    by_row = [
        jnp.sum(
            jnp.where(pick, by_pair[i * PER_ATOM : (i + 1) * PER_ATOM], 0.0),
            axis=0,
            keepdims=True,
        )
        for i in range(PER_ATOM)
    ]
    tiled = jnp.concatenate(by_row * atoms, axis=0)
    same_atom = (
        lax.broadcasted_iota(jnp.int32, (nproj, nproj), 0) // PER_ATOM
        == lax.broadcasted_iota(jnp.int32, (nproj, nproj), 1) // PER_ATOM
    )
    aug = jnp.where(same_atom, tiled, 0.0)
    aug_real = dot00(aug, proj_real, HIGHEST)
    aug_imag = dot00(aug, proj_imag, HIGHEST)

    sites = jnp.dot(sites_ref[...], spread, precision=HIGHEST, preferred_element_type=f32)
    chunks = rows // 128
    lanes = lax.broadcasted_iota(jnp.int32, (8, 128), 1)
    block = lax.broadcasted_iota(jnp.int32, (8, 128), 0)
    row_ids = block * 128 + lanes
    along_a = (row_ids % SIDE).astype(f32) / SIDE
    along_b = (row_ids // SIDE % SIDE).astype(f32) / SIDE
    along_c = (row_ids // (SIDE * SIDE)).astype(f32) / DEPTH

    for v in range(2):
        vector = v ^ place.swap
        first_hi = place.first_hi(v)
        q = [
            b_ref[vector, axis] + shift_ref[0, vector, axis].astype(f32)
            for axis in range(3)
        ]
        theta = TWO_PI * (q[0] * along_a + q[1] * along_b + q[2] * along_c)
        phi = TWO_PI * (q[0] * sites[0:1] + q[1] * sites[1:2] + q[2] * sites[2:3])
        angle = theta
        for part in range(nproj // 128):
            piece = phi[0:1, part * 128 : (part + 1) * 128]
            angle = jnp.where(block == chunks + part, piece, angle)
        cosine = jnp.transpose(jnp.cos(angle))
        sine = jnp.transpose(jnp.sin(angle))
        weights = []
        for part in range(nproj // 128):
            at = slice(part * 128, (part + 1) * 128)
            cos_p = cosine[:, chunks + part : chunks + part + 1]
            sin_p = sine[:, chunks + part : chunks + part + 1]
            weights.append(
                (
                    cos_p * aug_real[at] - sin_p * aug_imag[at],
                    cos_p * aug_imag[at] + sin_p * aug_real[at],
                )
            )
        weight_real = jnp.concatenate([w[0] for w in weights], axis=0)
        weight_imag = jnp.concatenate([w[1] for w in weights], axis=0)

        def spread_rows(weight):
            high = weight.astype(jnp.bfloat16)
            low = (weight - high.astype(f32)).astype(jnp.bfloat16)
            return jnp.dot(masked, high, preferred_element_type=f32) + jnp.dot(
                masked, low, preferred_element_type=f32
            )

        added_real = spread_rows(weight_real)
        added_imag = spread_rows(weight_imag)
        per_chunk = 128 // SLAB_ROWS
        for s in range(SLABS):
            chunk, inside = s // per_chunk, s % per_chunk * SLAB_ROWS
            at = slice(s * SLAB_ROWS, (s + 1) * SLAB_ROWS)
            cos_r = cosine[inside : inside + SLAB_ROWS, chunk : chunk + 1]
            sin_r = sine[inside : inside + SLAB_ROWS, chunk : chunk + 1]
            wave_real = real_ref[at, :].astype(f32)
            wave_imag = imag_ref[at, :].astype(f32)
            left_real = cos_r * wave_real - sin_r * wave_imag + added_real[at]
            left_imag = cos_r * wave_imag + sin_r * wave_real + added_imag[at]
            left_real = left_real.astype(jnp.bfloat16)
            left_imag = left_imag.astype(jnp.bfloat16)
            slab_hi, slab_x, slab_core = s // (CORE * X), s // CORE % X, s % CORE
            step = (slab_x - place.x) & (X - 1)
            piece = jnp.where(step == 3, 1, jnp.where(step == 0, 0, step + 1))
            slot = piece * 4 + (slab_hi ^ first_hi) * 2 + (slab_core ^ core)
            top, low = pl.ds(0, SLAB_ROWS), pl.ds(SLAB_ROWS, SLAB_ROWS)
            for side in range(2):
                real_half = left_real[:, side * width : (side + 1) * width]
                imag_half = left_imag[:, side * width : (side + 1) * width]
                base = side * 2 * width
                out_ref[v, slot, top, base : base + width] = real_half
                out_ref[v, slot, low, base : base + width] = imag_half
                out_ref[v, slot, top, base + width : base + 2 * width] = -imag_half
                out_ref[v, slot, low, base + width : base + 2 * width] = real_half


def left_operators(partner, b_vectors, shift, own, other, projectors, support, counts, aug, sites):
    rows, nproj = projectors.shape
    width = own.shape[2] // 2
    smem = pl.BlockSpec(memory_space=pltpu.SMEM)
    vmem = pl.BlockSpec(memory_space=pltpu.VMEM)
    return pl.pallas_call(
        left_kernel,
        out_shape=jax.ShapeDtypeStruct((2, SLABS, 2 * SLAB_ROWS, 4 * width), jnp.bfloat16),
        in_specs=[smem] * 3 + [vmem] * 7,
        out_specs=vmem,
        scratch_shapes=[
            pltpu.VMEM((rows, 2 * width), jnp.bfloat16),
            pltpu.VMEM((rows, 2 * width), jnp.bfloat16),
            pltpu.VMEM((rows, nproj), jnp.bfloat16),
            pltpu.VMEM((2,) + own.shape, jnp.bfloat16),
        ],
        compiler_params=pltpu.CompilerParams(vmem_limit_bytes=28 * 1024 * 1024),
        cost_estimate=pl.CostEstimate(
            flops=2_000_000_000, bytes_accessed=4 * 1024 * 1024, transcendentals=4096
        ),
        name="left_operators",
    )(partner, b_vectors, shift, own, other, projectors, support, counts, aug, sites)


def product_kernel(partner_ref, left_ref, held, from_left, from_right, far_left, far_right, out_ref):
    swap = Place(partner_ref).swap
    rows = held.shape[0] // 4
    for v in range(2):
        near, far = pl.ds(v * rows, rows), pl.ds((2 + v) * rows, rows)
        pieces = [ref[at, :] for ref in (held, from_left, from_right) for at in (near, far)]
        pieces = pieces + [far_left[near, :], far_right[near, :]]
        right = jnp.concatenate(pieces, axis=0)
        out_ref[v ^ swap] = dot00(left_ref[v], right).astype(jnp.bfloat16)


def products(partner, left, side, pieces):
    depth = left.shape[1]
    half = left.shape[2] // 2
    columns = pieces[0].shape[1]
    return pl.pallas_call(
        product_kernel,
        grid=(1,),
        out_shape=jax.ShapeDtypeStruct((2, half, columns), jnp.bfloat16),
        in_specs=[
            pl.BlockSpec(memory_space=pltpu.SMEM),
            pl.BlockSpec((2, depth, half), lambda i: (0, 0, side)),
        ]
        + [pl.BlockSpec(piece.shape, lambda i: (0, 0)) for piece in pieces],
        out_specs=pl.BlockSpec((2, half, columns), lambda i: (0, 0, 0)),
        compiler_params=pltpu.CompilerParams(vmem_limit_bytes=28 * 1024 * 1024),
        cost_estimate=pl.CostEstimate(
            flops=4 * depth * half * columns,
            bytes_accessed=7 * 1024 * 1024,
            transcendentals=0,
        ),
        name="products",
    )(partner, left, *pieces)


def body(
    wavefunctions,
    projectors,
    support,
    proj_counts,
    aug_matrices,
    atom_sites,
    b_vectors,
    partner,
    lattice_shift,
):
    waves = wavefunctions[0]
    row_count, _, bands = waves.shape
    half_bands = bands // CORE
    place = Place(partner)
    core, x, z_hi, distances = place.core, place.x, place.z_hi, place.distances

    slab = jnp.transpose(waves, (1, 0, 2)).reshape(2 * row_count, bands)
    low, high = slab[:, :half_bands], slab[:, half_bands:]
    kept = jnp.where(core == 0, low, high)
    given = jnp.where(core == 0, high, low)
    lane = jnp.concatenate([kept, from_other_core(given)], axis=0)
    half_rows = lane.shape[0]

    chip_bands = half_bands // X

    def bands_of(lane, offset):
        start = (x + offset) % X * chip_bands
        return lax.dynamic_slice_in_dim(lane, start, chip_bands, axis=1)

    def first_stage(distance, lane):
        onward = jnp.concatenate([bands_of(lane, 1), bands_of(lane, 2)], axis=0)
        return (
            toward_partner(lane, distance),
            from_x(onward, -1),
            from_x(bands_of(lane, -1), 1),
        )

    def second_stage(distance, lane, moved_first, onward):
        held_first = both_halves(moved_first)
        return (
            toward_partner(lane, distance),
            held_first,
            from_x(onward[half_rows:], -1),
        )

    moved_first, one_back, one_on = lax.switch(
        distances[0],
        [functools.partial(first_stage, d) for d in range(POINTS)],
        lane,
    )
    moved_second, held_first, two_back = lax.switch(
        distances[1],
        [functools.partial(second_stage, d) for d in range(POINTS)],
        lane,
        moved_first,
        one_back,
    )
    held_second = both_halves(moved_second)
    held = jnp.concatenate(
        [held_first[0], held_second[0], held_first[1], held_second[1]], axis=0
    )
    from_left, from_right = from_x(held, -1), from_x(held, 1)
    far_left = from_x(from_left[: 2 * half_rows], -1)
    far_right = from_x(from_right[2 * half_rows :], 1)
    own = jnp.concatenate([bands_of(lane, 0), one_back[:half_rows], two_back, one_on], axis=0)
    own = jnp.where(core == z_hi, own, from_other_half(own))
    other = from_other_core(own)
    own_shape = (X * CORE, 2 * row_count, chip_bands)
    own, other = own.reshape(own_shape), other.reshape(own_shape)
    left = left_operators(
        partner,
        b_vectors,
        lattice_shift,
        own,
        other,
        projectors,
        jnp.transpose(support),
        proj_counts.reshape(1, -1),
        jnp.transpose(aug_matrices, (1, 2, 0)).reshape(-1, support.shape[0]),
        jnp.transpose(atom_sites),
    )
    left = left.reshape(2, left.shape[1] * left.shape[2], left.shape[3])

    pieces = (held, from_left, from_right, far_left, far_right)
    theirs = products(partner, left, 1, pieces)
    got = from_other_core(theirs)
    mine = products(partner, left, 0, pieces)
    final = jnp.concatenate(
        [jnp.where(core == 0, mine, got), jnp.where(core == 0, got, mine)], axis=2
    )
    return final.reshape(1, 2, 2, bands // SLABS, bands)


def solution(mesh):
    in_specs = (
        P("ka", "grid", None, None),
        P(),
        P(),
        P(),
        P(),
        P(),
        P(),
        P("ka", None),
        P("ka", None, None),
    )
    out_specs = P("ka", None, None, "grid", None)
    return jax.shard_map(body, mesh=mesh, in_specs=in_specs, out_specs=out_specs, check_vma=False)
```

```python
import functools
import math

import jax
import jax.numpy as jnp
from jax import lax
from jax.experimental import pallas as pl
from jax.experimental.pallas import tpu as pltpu
from jax.sharding import PartitionSpec as P

SIDE = 16
DEPTH = 96
TWO_PI = 2.0 * math.pi

Z_LO, Y, Z_HI, X, CORE = 4, 8, 2, 4, 2
Z = Z_LO * Z_HI
POINTS = Z_LO * Y
AXES = ("ka", "grid")
SLABS = 16
SLAB_ROWS = 32
PER_ATOM = 8
HIGHEST = lax.Precision.HIGHEST


def flat_id(x, y, z, core):
    return (((z % Z_LO) * Y + y) * Z_HI + z // Z_LO) * (X * CORE) + x * CORE + core


def route(source_of):
    pairs = []
    for x in range(X):
        for y in range(Y):
            for z in range(Z):
                for core in range(CORE):
                    source = source_of(x, y, z, core)
                    if source is None:
                        continue
                    sx, sy, sz, sc = source
                    pairs.append(
                        (flat_id(sx % X, sy % Y, sz % Z, sc), flat_id(x, y, z, core))
                    )
    return pairs


def moved(block, source_of):
    return lax.ppermute(block, AXES, route(source_of))


def from_other_core(block):
    return moved(block, lambda x, y, z, core: (x, y, z, 1 - core))


def from_x(block, offset):
    return moved(block, lambda x, y, z, core: (x + offset, y, z, core))


def z_offset(distance, core, y):
    part = (distance // Y + 2 + (y + distance % Y) // Y) % Z_LO
    other_way = (part == 2) * core * (distance % Y != 0)
    return part - Z_LO * (part == 3) - Z_LO * other_way


class Place:
    def __init__(self, partner):
        point, member = lax.axis_index("ka"), lax.axis_index("grid")
        self.core = member & (CORE - 1)
        self.x = (member >> 1) & (X - 1)
        self.z_hi = member >> 3
        self.y = point & (Y - 1)
        self.z = self.z_hi * Z_LO + (point >> 3)
        distances = [(partner[0, v] - point) & (POINTS - 1) for v in range(2)]
        along = [d & (Y - 1) for d in distances]
        hops = [jnp.where(d == Y // 2, 2, jnp.minimum(d, Y - d)) for d in along]
        swapped = hops[0] > hops[1]
        self.swap = jnp.where(swapped, 1, 0)
        self.distances = [
            jnp.where(swapped, distances[1 - v], distances[v]) for v in range(2)
        ]

    def first_hi(self, v):
        distance = self.distances[v]
        along = distance & (Y - 1)
        part = ((distance >> 3) + 2 + ((self.y + along) >> 3)) & (Z_LO - 1)
        other_way = (part == 2) & (self.core == 1) & (along != 0)
        back = jnp.where((part == 3) | other_way, Z_LO, 0)
        return ((self.z - 2 + part - back) & (Z - 1)) >> 2


def from_other_half(block):
    return moved(
        block,
        lambda x, y, z, core: None if core == z // Z_LO else (x, y, z + Z_LO, 1 - core),
    )


def toward_partner(lane, distance):
    def source(x, y, z, core):
        return x, (y + distance) % Y, z + z_offset(distance, core, y), core

    if all(source(0, y, 0, c) == (0, y, 0, c) for y in range(Y) for c in range(CORE)):
        return lane
    return moved(lane, source)


def both_halves(lane):
    behind = moved(lane, lambda x, y, z, core: (x, y, z - 2, core))
    ahead = moved(lane, lambda x, y, z, core: (x, y, z + 2, core))
    return behind, ahead


def dot00(left, right, precision=None):
    return lax.dot_general(
        left,
        right,
        (((0,), (0,)), ((), ())),
        precision=precision,
        preferred_element_type=jnp.float32,
    )


def left_kernel(
    partner_ref,
    b_ref,
    shift_ref,
    own_ref,
    other_ref,
    proj_ref,
    support_ref,
    counts_ref,
    aug_ref,
    sites_ref,
    out_ref,
    real_ref,
    imag_ref,
    masked_ref,
    both_ref,
):
    atoms = support_ref.shape[1]
    nproj = proj_ref.shape[1]
    rows = proj_ref.shape[0]
    width = own_ref.shape[2] // 2
    place = Place(partner_ref)
    core = place.core
    f32 = jnp.float32

    atom_of = lax.broadcasted_iota(jnp.int32, (atoms, nproj), 1) // PER_ATOM
    spread = (atom_of == lax.broadcasted_iota(jnp.int32, (atoms, nproj), 0)).astype(f32)
    reach = jnp.dot(support_ref[...].astype(f32), spread, preferred_element_type=f32)
    counts = jnp.broadcast_to(counts_ref[...].astype(f32), (8, atoms))
    counts = jnp.dot(counts, spread, preferred_element_type=f32)[0:1]
    slot_id = (lax.broadcasted_iota(jnp.int32, (1, nproj), 1) % PER_ATOM).astype(f32)
    keep = reach * (slot_id < counts - 0.5).astype(f32)
    both_ref[core] = own_ref[...]
    both_ref[1 - core] = other_ref[...]
    for s in range(SLABS):
        at = pl.ds(s * SLAB_ROWS, SLAB_ROWS)
        masked_ref[at, :] = (proj_ref[at, :].astype(f32) * keep[s : s + 1, :]).astype(
            jnp.bfloat16
        )
        slab_hi, slab_x, slab_core = s // (CORE * X), s // CORE % X, s % CORE
        slab = CORE * ((place.x - slab_x) & (X - 1)) + (slab_core ^ place.z_hi)
        for side in range(2):
            lanes = pl.ds(pl.multiple_of((core ^ side) * width, width), width)
            to = pl.ds(side * width, width)
            real_ref[at, to] = both_ref[slab_hi, slab, pl.ds(0, SLAB_ROWS), lanes]
            imag_ref[at, to] = both_ref[slab_hi, slab, pl.ds(SLAB_ROWS, SLAB_ROWS), lanes]

    masked = masked_ref[...]
    proj_real = dot00(masked, real_ref[...]).astype(jnp.bfloat16).astype(f32)
    proj_imag = dot00(masked, imag_ref[...]).astype(jnp.bfloat16).astype(f32)

    by_pair = jnp.dot(aug_ref[...], spread, precision=HIGHEST, preferred_element_type=f32)
    column = lax.broadcasted_iota(jnp.int32, (PER_ATOM, nproj), 1) % PER_ATOM
    pick = column == lax.broadcasted_iota(jnp.int32, (PER_ATOM, nproj), 0)
    by_row = [
        jnp.sum(
            jnp.where(pick, by_pair[i * PER_ATOM : (i + 1) * PER_ATOM], 0.0),
            axis=0,
            keepdims=True,
        )
        for i in range(PER_ATOM)
    ]
    tiled = jnp.concatenate(by_row * atoms, axis=0)
    same_atom = (
        lax.broadcasted_iota(jnp.int32, (nproj, nproj), 0) // PER_ATOM
        == lax.broadcasted_iota(jnp.int32, (nproj, nproj), 1) // PER_ATOM
    )
    aug = jnp.where(same_atom, tiled, 0.0)
    aug_real = dot00(aug, proj_real, HIGHEST)
    aug_imag = dot00(aug, proj_imag, HIGHEST)

    sites = jnp.dot(sites_ref[...], spread, precision=HIGHEST, preferred_element_type=f32)
    chunks = rows // 128
    lanes = lax.broadcasted_iota(jnp.int32, (8, 128), 1)
    block = lax.broadcasted_iota(jnp.int32, (8, 128), 0)
    row_ids = block * 128 + lanes
    along_a = (row_ids % SIDE).astype(f32) / SIDE
    along_b = (row_ids // SIDE % SIDE).astype(f32) / SIDE
    along_c = (row_ids // (SIDE * SIDE)).astype(f32) / DEPTH

    for v in range(2):
        vector = v ^ place.swap
        first_hi = place.first_hi(v)
        q = [
            b_ref[vector, axis] + shift_ref[0, vector, axis].astype(f32)
            for axis in range(3)
        ]
        theta = TWO_PI * (q[0] * along_a + q[1] * along_b + q[2] * along_c)
        phi = TWO_PI * (q[0] * sites[0:1] + q[1] * sites[1:2] + q[2] * sites[2:3])
        angle = theta
        for part in range(nproj // 128):
            piece = phi[0:1, part * 128 : (part + 1) * 128]
            angle = jnp.where(block == chunks + part, piece, angle)
        cosine = jnp.transpose(jnp.cos(angle))
        sine = jnp.transpose(jnp.sin(angle))
        weights = []
        for part in range(nproj // 128):
            at = slice(part * 128, (part + 1) * 128)
            cos_p = cosine[:, chunks + part : chunks + part + 1]
            sin_p = sine[:, chunks + part : chunks + part + 1]
            weights.append(
                (
                    cos_p * aug_real[at] - sin_p * aug_imag[at],
                    cos_p * aug_imag[at] + sin_p * aug_real[at],
                )
            )
        weight_real = jnp.concatenate([w[0] for w in weights], axis=0)
        weight_imag = jnp.concatenate([w[1] for w in weights], axis=0)

        def spread_rows(weight):
            high = weight.astype(jnp.bfloat16)
            low = (weight - high.astype(f32)).astype(jnp.bfloat16)
            return jnp.dot(masked, high, preferred_element_type=f32) + jnp.dot(
                masked, low, preferred_element_type=f32
            )

        added_real = spread_rows(weight_real)
        added_imag = spread_rows(weight_imag)
        per_chunk = 128 // SLAB_ROWS
        for s in range(SLABS):
            chunk, inside = s // per_chunk, s % per_chunk * SLAB_ROWS
            at = slice(s * SLAB_ROWS, (s + 1) * SLAB_ROWS)
            cos_r = cosine[inside : inside + SLAB_ROWS, chunk : chunk + 1]
            sin_r = sine[inside : inside + SLAB_ROWS, chunk : chunk + 1]
            wave_real = real_ref[at, :].astype(f32)
            wave_imag = imag_ref[at, :].astype(f32)
            left_real = cos_r * wave_real - sin_r * wave_imag + added_real[at]
            left_imag = cos_r * wave_imag + sin_r * wave_real + added_imag[at]
            left_real = left_real.astype(jnp.bfloat16)
            left_imag = left_imag.astype(jnp.bfloat16)
            slab_hi, slab_x, slab_core = s // (CORE * X), s // CORE % X, s % CORE
            step = (slab_x - place.x) & (X - 1)
            piece = jnp.where(step == 3, 1, jnp.where(step == 0, 0, step + 1))
            slot = piece * 4 + (slab_hi ^ first_hi) * 2 + (slab_core ^ core)
            top, low = pl.ds(0, SLAB_ROWS), pl.ds(SLAB_ROWS, SLAB_ROWS)
            for side in range(2):
                real_half = left_real[:, side * width : (side + 1) * width]
                imag_half = left_imag[:, side * width : (side + 1) * width]
                base = side * 2 * width
                out_ref[v, slot, top, base : base + width] = real_half
                out_ref[v, slot, low, base : base + width] = imag_half
                out_ref[v, slot, top, base + width : base + 2 * width] = -imag_half
                out_ref[v, slot, low, base + width : base + 2 * width] = real_half


def left_operators(partner, b_vectors, shift, own, other, projectors, support, counts, aug, sites):
    rows, nproj = projectors.shape
    width = own.shape[2] // 2
    smem = pl.BlockSpec(memory_space=pltpu.SMEM)
    vmem = pl.BlockSpec(memory_space=pltpu.VMEM)
    return pl.pallas_call(
        left_kernel,
        out_shape=jax.ShapeDtypeStruct((2, SLABS, 2 * SLAB_ROWS, 4 * width), jnp.bfloat16),
        in_specs=[smem] * 3 + [vmem] * 7,
        out_specs=vmem,
        scratch_shapes=[
            pltpu.VMEM((rows, 2 * width), jnp.bfloat16),
            pltpu.VMEM((rows, 2 * width), jnp.bfloat16),
            pltpu.VMEM((rows, nproj), jnp.bfloat16),
            pltpu.VMEM((2,) + own.shape, jnp.bfloat16),
        ],
        compiler_params=pltpu.CompilerParams(vmem_limit_bytes=28 * 1024 * 1024),
        cost_estimate=pl.CostEstimate(
            flops=2_000_000_000, bytes_accessed=4 * 1024 * 1024, transcendentals=4096
        ),
        name="left_operators",
    )(partner, b_vectors, shift, own, other, projectors, support, counts, aug, sites)


def product_kernel(partner_ref, left_ref, held, from_left, from_right, far_left, far_right, out_ref):
    swap = Place(partner_ref).swap
    rows = held.shape[0] // 4
    for v in range(2):
        near, far = pl.ds(v * rows, rows), pl.ds((2 + v) * rows, rows)
        pieces = [ref[at, :] for ref in (held, from_left, from_right) for at in (near, far)]
        pieces = pieces + [far_left[near, :], far_right[near, :]]
        right = jnp.concatenate(pieces, axis=0)
        out_ref[v ^ swap] = dot00(left_ref[v], right).astype(jnp.bfloat16)


def products(partner, left, side, pieces):
    depth = left.shape[1]
    half = left.shape[2] // 2
    columns = pieces[0].shape[1]
    return pl.pallas_call(
        product_kernel,
        grid=(1,),
        out_shape=jax.ShapeDtypeStruct((2, half, columns), jnp.bfloat16),
        in_specs=[
            pl.BlockSpec(memory_space=pltpu.SMEM),
            pl.BlockSpec((2, depth, half), lambda i: (0, 0, side)),
        ]
        + [pl.BlockSpec(piece.shape, lambda i: (0, 0)) for piece in pieces],
        out_specs=pl.BlockSpec((2, half, columns), lambda i: (0, 0, 0)),
        compiler_params=pltpu.CompilerParams(vmem_limit_bytes=28 * 1024 * 1024),
        cost_estimate=pl.CostEstimate(
            flops=4 * depth * half * columns,
            bytes_accessed=7 * 1024 * 1024,
            transcendentals=0,
        ),
        name="products",
    )(partner, left, *pieces)


def body(
    wavefunctions,
    projectors,
    support,
    proj_counts,
    aug_matrices,
    atom_sites,
    b_vectors,
    partner,
    lattice_shift,
):
    waves = wavefunctions[0]
    row_count, _, bands = waves.shape
    half_bands = bands // CORE
    place = Place(partner)
    core, x, z_hi, distances = place.core, place.x, place.z_hi, place.distances

    slab = jnp.transpose(waves, (1, 0, 2)).reshape(2 * row_count, bands)
    low, high = slab[:, :half_bands], slab[:, half_bands:]
    kept = jnp.where(core == 0, low, high)
    given = jnp.where(core == 0, high, low)
    lane = jnp.concatenate([kept, from_other_core(given)], axis=0)
    half_rows = lane.shape[0]

    chip_bands = half_bands // X

    def bands_of(lane, offset):
        start = (x + offset) % X * chip_bands
        return lax.dynamic_slice_in_dim(lane, start, chip_bands, axis=1)

    def first_stage(distance, lane):
        onward = jnp.concatenate([bands_of(lane, 1), bands_of(lane, 2)], axis=0)
        return (
            toward_partner(lane, distance),
            from_x(onward, -1),
            from_x(bands_of(lane, -1), 1),
        )

    def second_stage(distance, lane, moved_first, onward):
        held_first = both_halves(moved_first)
        return (
            toward_partner(lane, distance),
            held_first,
            from_x(onward, -1),
        )

    moved_first, one_back, one_on = lax.switch(
        distances[0],
        [functools.partial(first_stage, d) for d in range(POINTS)],
        lane,
    )
    moved_second, held_first, two_back = lax.switch(
        distances[1],
        [functools.partial(second_stage, d) for d in range(POINTS)],
        lane,
        moved_first,
        one_back,
    )
    held_second = both_halves(moved_second)
    held = jnp.concatenate(
        [held_first[0], held_second[0], held_first[1], held_second[1]], axis=0
    )
    from_left, from_right = from_x(held, -1), from_x(held, 1)
    far_left = from_x(from_left[: 2 * half_rows], -1)
    far_right = from_x(from_right[2 * half_rows :], 1)
    own = jnp.concatenate(
        [bands_of(lane, 0), one_back[:half_rows], two_back[half_rows:], one_on], axis=0
    )
    own = jnp.where(core == z_hi, own, from_other_half(own))
    other = from_other_core(own)
    own_shape = (X * CORE, 2 * row_count, chip_bands)
    own, other = own.reshape(own_shape), other.reshape(own_shape)
    left = left_operators(
        partner,
        b_vectors,
        lattice_shift,
        own,
        other,
        projectors,
        jnp.transpose(support),
        proj_counts.reshape(1, -1),
        jnp.transpose(aug_matrices, (1, 2, 0)).reshape(-1, support.shape[0]),
        jnp.transpose(atom_sites),
    )
    left = left.reshape(2, left.shape[1] * left.shape[2], left.shape[3])

    pieces = (held, from_left, from_right, far_left, far_right)
    theirs = products(partner, left, 1, pieces)
    got = from_other_core(theirs)
    mine = products(partner, left, 0, pieces)
    final = jnp.concatenate(
        [jnp.where(core == 0, mine, got), jnp.where(core == 0, got, mine)], axis=2
    )
    return final.reshape(1, 2, 2, bands // SLABS, bands)


def solution(mesh):
    in_specs = (
        P("ka", "grid", None, None),
        P(),
        P(),
        P(),
        P(),
        P(),
        P(),
        P("ka", None),
        P("ka", None, None),
    )
    out_specs = P("ka", None, None, "grid", None)
    return jax.shard_map(body, mesh=mesh, in_specs=in_specs, out_specs=out_specs, check_vma=False)
```

```python
import functools
import math

import jax
import jax.numpy as jnp
from jax import lax
from jax.experimental import pallas as pl
from jax.experimental.pallas import tpu as pltpu
from jax.sharding import PartitionSpec as P

SIDE = 16
DEPTH = 96
TWO_PI = 2.0 * math.pi

Z_LO, Y, Z_HI, X, CORE = 4, 8, 2, 4, 2
Z = Z_LO * Z_HI
POINTS = Z_LO * Y
AXES = ("ka", "grid")
SLABS = 16
SLAB_ROWS = 32
PER_ATOM = 8
HIGHEST = lax.Precision.HIGHEST


def flat_id(x, y, z, core):
    return (((z % Z_LO) * Y + y) * Z_HI + z // Z_LO) * (X * CORE) + x * CORE + core


def route(source_of):
    pairs = []
    for x in range(X):
        for y in range(Y):
            for z in range(Z):
                for core in range(CORE):
                    sx, sy, sz, sc = source_of(x, y, z, core)
                    pairs.append(
                        (flat_id(sx % X, sy % Y, sz % Z, sc), flat_id(x, y, z, core))
                    )
    return pairs


def moved(block, source_of):
    return lax.ppermute(block, AXES, route(source_of))


def from_other_core(block):
    return moved(block, lambda x, y, z, core: (x, y, z, 1 - core))


def from_x(block, offset):
    return moved(block, lambda x, y, z, core: (x + offset, y, z, core))


def z_offset(distance, core, y):
    part = (distance // Y + 2 + (y + distance % Y) // Y) % Z_LO
    other_way = (part == 2) * core * (distance % Y != 0)
    return part - Z_LO * (part == 3) - Z_LO * other_way


class Place:
    def __init__(self, partner):
        point, member = lax.axis_index("ka"), lax.axis_index("grid")
        self.core = member & (CORE - 1)
        self.x = (member >> 1) & (X - 1)
        self.z_hi = member >> 3
        self.y = point & (Y - 1)
        self.z = self.z_hi * Z_LO + (point >> 3)
        distances = [(partner[0, v] - point) & (POINTS - 1) for v in range(2)]
        along = [d & (Y - 1) for d in distances]
        hops = [jnp.where(d == Y // 2, 2, jnp.minimum(d, Y - d)) for d in along]
        swapped = hops[0] > hops[1]
        self.swap = jnp.where(swapped, 1, 0)
        self.distances = [
            jnp.where(swapped, distances[1 - v], distances[v]) for v in range(2)
        ]

    def first_hi(self, v):
        distance = self.distances[v]
        along = distance & (Y - 1)
        part = ((distance >> 3) + 2 + ((self.y + along) >> 3)) & (Z_LO - 1)
        other_way = (part == 2) & (self.core == 1) & (along != 0)
        back = jnp.where((part == 3) | other_way, Z_LO, 0)
        return ((self.z - 2 + part - back) & (Z - 1)) >> 2


def from_other_half(block):
    return moved(block, lambda x, y, z, core: (x, y, z + Z_LO, core))


def toward_partner(lane, distance):
    def source(x, y, z, core):
        return x, (y + distance) % Y, z + z_offset(distance, core, y), core

    if all(source(0, y, 0, c) == (0, y, 0, c) for y in range(Y) for c in range(CORE)):
        return lane
    return moved(lane, source)


def both_halves(lane):
    behind = moved(lane, lambda x, y, z, core: (x, y, z - 2, core))
    ahead = moved(lane, lambda x, y, z, core: (x, y, z + 2, core))
    return behind, ahead


def dot00(left, right, precision=None):
    return lax.dot_general(
        left,
        right,
        (((0,), (0,)), ((), ())),
        precision=precision,
        preferred_element_type=jnp.float32,
    )


def left_kernel(
    partner_ref,
    b_ref,
    shift_ref,
    own_ref,
    other_ref,
    proj_ref,
    support_ref,
    counts_ref,
    aug_ref,
    sites_ref,
    out_ref,
    real_ref,
    imag_ref,
    masked_ref,
    both_ref,
):
    atoms = support_ref.shape[1]
    nproj = proj_ref.shape[1]
    rows = proj_ref.shape[0]
    width = own_ref.shape[2] // 2
    place = Place(partner_ref)
    core = place.core
    f32 = jnp.float32

    atom_of = lax.broadcasted_iota(jnp.int32, (atoms, nproj), 1) // PER_ATOM
    spread = (atom_of == lax.broadcasted_iota(jnp.int32, (atoms, nproj), 0)).astype(f32)
    reach = jnp.dot(support_ref[...].astype(f32), spread, preferred_element_type=f32)
    counts = jnp.broadcast_to(counts_ref[...].astype(f32), (8, atoms))
    counts = jnp.dot(counts, spread, preferred_element_type=f32)[0:1]
    slot_id = (lax.broadcasted_iota(jnp.int32, (1, nproj), 1) % PER_ATOM).astype(f32)
    keep = reach * (slot_id < counts - 0.5).astype(f32)
    both_ref[core] = own_ref[...]
    both_ref[1 - core] = other_ref[...]
    for s in range(SLABS):
        at = pl.ds(s * SLAB_ROWS, SLAB_ROWS)
        masked_ref[at, :] = (proj_ref[at, :].astype(f32) * keep[s : s + 1, :]).astype(
            jnp.bfloat16
        )
        slab_hi, slab_x, slab_core = s // (CORE * X), s // CORE % X, s % CORE
        slab = X * (slab_hi ^ place.z_hi) + ((place.x - slab_x) & (X - 1))
        for side in range(2):
            lanes = pl.ds(pl.multiple_of((core ^ side) * width, width), width)
            to = pl.ds(side * width, width)
            real_ref[at, to] = both_ref[slab_core, slab, pl.ds(0, SLAB_ROWS), lanes]
            imag_ref[at, to] = both_ref[slab_core, slab, pl.ds(SLAB_ROWS, SLAB_ROWS), lanes]

    masked = masked_ref[...]
    proj_real = dot00(masked, real_ref[...]).astype(jnp.bfloat16).astype(f32)
    proj_imag = dot00(masked, imag_ref[...]).astype(jnp.bfloat16).astype(f32)

    by_pair = jnp.dot(aug_ref[...], spread, precision=HIGHEST, preferred_element_type=f32)
    column = lax.broadcasted_iota(jnp.int32, (PER_ATOM, nproj), 1) % PER_ATOM
    pick = column == lax.broadcasted_iota(jnp.int32, (PER_ATOM, nproj), 0)
    by_row = [
        jnp.sum(
            jnp.where(pick, by_pair[i * PER_ATOM : (i + 1) * PER_ATOM], 0.0),
            axis=0,
            keepdims=True,
        )
        for i in range(PER_ATOM)
    ]
    tiled = jnp.concatenate(by_row * atoms, axis=0)
    same_atom = (
        lax.broadcasted_iota(jnp.int32, (nproj, nproj), 0) // PER_ATOM
        == lax.broadcasted_iota(jnp.int32, (nproj, nproj), 1) // PER_ATOM
    )
    aug = jnp.where(same_atom, tiled, 0.0)
    aug_real = dot00(aug, proj_real, HIGHEST)
    aug_imag = dot00(aug, proj_imag, HIGHEST)

    sites = jnp.dot(sites_ref[...], spread, precision=HIGHEST, preferred_element_type=f32)
    chunks = rows // 128
    lanes = lax.broadcasted_iota(jnp.int32, (8, 128), 1)
    block = lax.broadcasted_iota(jnp.int32, (8, 128), 0)
    row_ids = block * 128 + lanes
    along_a = (row_ids % SIDE).astype(f32) / SIDE
    along_b = (row_ids // SIDE % SIDE).astype(f32) / SIDE
    along_c = (row_ids // (SIDE * SIDE)).astype(f32) / DEPTH

    for v in range(2):
        vector = v ^ place.swap
        first_hi = place.first_hi(v)
        q = [
            b_ref[vector, axis] + shift_ref[0, vector, axis].astype(f32)
            for axis in range(3)
        ]
        theta = TWO_PI * (q[0] * along_a + q[1] * along_b + q[2] * along_c)
        phi = TWO_PI * (q[0] * sites[0:1] + q[1] * sites[1:2] + q[2] * sites[2:3])
        angle = theta
        for part in range(nproj // 128):
            piece = phi[0:1, part * 128 : (part + 1) * 128]
            angle = jnp.where(block == chunks + part, piece, angle)
        cosine = jnp.transpose(jnp.cos(angle))
        sine = jnp.transpose(jnp.sin(angle))
        weights = []
        for part in range(nproj // 128):
            at = slice(part * 128, (part + 1) * 128)
            cos_p = cosine[:, chunks + part : chunks + part + 1]
            sin_p = sine[:, chunks + part : chunks + part + 1]
            weights.append(
                (
                    cos_p * aug_real[at] - sin_p * aug_imag[at],
                    cos_p * aug_imag[at] + sin_p * aug_real[at],
                )
            )
        weight_real = jnp.concatenate([w[0] for w in weights], axis=0)
        weight_imag = jnp.concatenate([w[1] for w in weights], axis=0)

        def spread_rows(weight):
            high = weight.astype(jnp.bfloat16)
            low = (weight - high.astype(f32)).astype(jnp.bfloat16)
            return jnp.dot(masked, high, preferred_element_type=f32) + jnp.dot(
                masked, low, preferred_element_type=f32
            )

        added_real = spread_rows(weight_real)
        added_imag = spread_rows(weight_imag)
        per_chunk = 128 // SLAB_ROWS
        for s in range(SLABS):
            chunk, inside = s // per_chunk, s % per_chunk * SLAB_ROWS
            at = slice(s * SLAB_ROWS, (s + 1) * SLAB_ROWS)
            cos_r = cosine[inside : inside + SLAB_ROWS, chunk : chunk + 1]
            sin_r = sine[inside : inside + SLAB_ROWS, chunk : chunk + 1]
            wave_real = real_ref[at, :].astype(f32)
            wave_imag = imag_ref[at, :].astype(f32)
            left_real = cos_r * wave_real - sin_r * wave_imag + added_real[at]
            left_imag = cos_r * wave_imag + sin_r * wave_real + added_imag[at]
            left_real = left_real.astype(jnp.bfloat16)
            left_imag = left_imag.astype(jnp.bfloat16)
            slab_hi, slab_x, slab_core = s // (CORE * X), s // CORE % X, s % CORE
            step = (slab_x - place.x) & (X - 1)
            piece = jnp.where(step == 3, 1, jnp.where(step == 0, 0, step + 1))
            slot = piece * 4 + (slab_hi ^ first_hi) * 2 + (slab_core ^ core)
            top, low = pl.ds(0, SLAB_ROWS), pl.ds(SLAB_ROWS, SLAB_ROWS)
            for side in range(2):
                real_half = left_real[:, side * width : (side + 1) * width]
                imag_half = left_imag[:, side * width : (side + 1) * width]
                base = side * 2 * width
                out_ref[v, slot, top, base : base + width] = real_half
                out_ref[v, slot, low, base : base + width] = imag_half
                out_ref[v, slot, top, base + width : base + 2 * width] = -imag_half
                out_ref[v, slot, low, base + width : base + 2 * width] = real_half


def left_operators(partner, b_vectors, shift, own, other, projectors, support, counts, aug, sites):
    rows, nproj = projectors.shape
    width = own.shape[2] // 2
    smem = pl.BlockSpec(memory_space=pltpu.SMEM)
    vmem = pl.BlockSpec(memory_space=pltpu.VMEM)
    return pl.pallas_call(
        left_kernel,
        out_shape=jax.ShapeDtypeStruct((2, SLABS, 2 * SLAB_ROWS, 4 * width), jnp.bfloat16),
        in_specs=[smem] * 3 + [vmem] * 7,
        out_specs=vmem,
        scratch_shapes=[
            pltpu.VMEM((rows, 2 * width), jnp.bfloat16),
            pltpu.VMEM((rows, 2 * width), jnp.bfloat16),
            pltpu.VMEM((rows, nproj), jnp.bfloat16),
            pltpu.VMEM((2,) + own.shape, jnp.bfloat16),
        ],
        compiler_params=pltpu.CompilerParams(vmem_limit_bytes=28 * 1024 * 1024),
        cost_estimate=pl.CostEstimate(
            flops=2_000_000_000, bytes_accessed=4 * 1024 * 1024, transcendentals=4096
        ),
        name="left_operators",
    )(partner, b_vectors, shift, own, other, projectors, support, counts, aug, sites)


def near_rows(v, held, from_left, from_right):
    rows = held.shape[0] // 2
    return [ref[v * rows : (v + 1) * rows, :] for ref in (held, from_left, from_right)]


def far_rows(v, far_left, far_right):
    rows = far_left.shape[0] // 2
    return [ref[v * rows : (v + 1) * rows, :] for ref in (far_left, far_right)]


def theirs_near_kernel(left_ref, held, from_left, from_right, total_ref):
    half = left_ref.shape[2] // 2
    for v in range(2):
        right = jnp.concatenate(near_rows(v, held, from_left, from_right), axis=0)
        total_ref[v] = dot00(left_ref[v, : right.shape[0], half:], right)


def theirs_far_kernel(partner_ref, left_ref, total_ref, far_left, far_right, out_ref):
    swap = Place(partner_ref).swap
    half = left_ref.shape[2] // 2
    for v in range(2):
        right = jnp.concatenate(far_rows(v, far_left, far_right), axis=0)
        last = dot00(left_ref[v, -right.shape[0] :, half:], right)
        out_ref[v ^ swap] = (total_ref[v] + last).astype(jnp.bfloat16)


def mine_kernel(partner_ref, left_ref, held, from_left, from_right, far_left, far_right, out_ref):
    swap = Place(partner_ref).swap
    half = left_ref.shape[2] // 2
    for v in range(2):
        pieces = near_rows(v, held, from_left, from_right) + far_rows(v, far_left, far_right)
        right = jnp.concatenate(pieces, axis=0)
        out_ref[v ^ swap] = dot00(left_ref[v, :, :half], right).astype(jnp.bfloat16)


def product(kernel, dtype, depth, *operands, partner=None):
    left, columns = operands[0], operands[-1].shape[1]
    half = left.shape[2] // 2
    smem = pl.BlockSpec(memory_space=pltpu.SMEM)
    vmem = pl.BlockSpec(memory_space=pltpu.VMEM)
    first = () if partner is None else (partner,)
    return pl.pallas_call(
        kernel,
        out_shape=jax.ShapeDtypeStruct((2, half, columns), dtype),
        in_specs=[smem] * len(first) + [vmem] * len(operands),
        out_specs=vmem,
        compiler_params=pltpu.CompilerParams(vmem_limit_bytes=28 * 1024 * 1024),
        cost_estimate=pl.CostEstimate(
            flops=4 * depth * half * columns,
            bytes_accessed=1024 * 1024,
            transcendentals=0,
        ),
        name="product",
    )(*first, *operands)


def body(
    wavefunctions,
    projectors,
    support,
    proj_counts,
    aug_matrices,
    atom_sites,
    b_vectors,
    partner,
    lattice_shift,
):
    waves = wavefunctions[0]
    row_count, _, bands = waves.shape
    half_bands = bands // CORE
    place = Place(partner)
    core, x, z_hi, distances = place.core, place.x, place.z_hi, place.distances

    slab = jnp.transpose(waves, (1, 0, 2)).reshape(2 * row_count, bands)
    low, high = slab[:, :half_bands], slab[:, half_bands:]
    kept = jnp.where(core == 0, low, high)
    given = jnp.where(core == 0, high, low)
    lane = jnp.concatenate([kept, from_other_core(given)], axis=0)
    half_rows = lane.shape[0]

    chip_bands = half_bands // X

    def bands_of(offset):
        blocks = [
            lax.dynamic_slice_in_dim(
                slab, (half * X + ((x + offset) & (X - 1))) * chip_bands, chip_bands, axis=1
            )
            for half in (z_hi, 1 - z_hi)
        ]
        return jnp.concatenate(blocks, axis=0)

    def first_stage(distance, lane):
        onward = jnp.concatenate([bands_of(1), bands_of(2)], axis=0)
        return (
            toward_partner(lane, distance),
            from_x(onward, -1),
            from_x(bands_of(-1), 1),
        )

    def second_stage(distance, lane, moved_first, onward):
        held_first = both_halves(moved_first)
        return (
            toward_partner(lane, distance),
            held_first,
            from_x(onward, -1),
        )

    moved_first, one_back, one_on = lax.switch(
        distances[0],
        [functools.partial(first_stage, d) for d in range(POINTS)],
        lane,
    )
    moved_second, held_first, two_back = lax.switch(
        distances[1],
        [functools.partial(second_stage, d) for d in range(POINTS)],
        lane,
        moved_first,
        one_back,
    )
    held_second = both_halves(moved_second)
    held = jnp.concatenate([*held_first, *held_second], axis=0)
    from_left, from_right = from_x(held, -1), from_x(held, 1)

    def of_both(block, half):
        rows = [block[i * half_rows : (i + 1) * half_rows] for i in (half, 2 + half)]
        return jnp.concatenate(rows, axis=0)

    far_left = from_x(of_both(from_left, 0), -1)
    far_right = from_x(of_both(from_right, 1), 1)
    along_x = (bands_of(0), one_back[:half_rows], two_back[half_rows:], one_on)
    slab_rows = 2 * row_count
    blocks = jnp.concatenate(along_x, axis=0).reshape(X, Z_HI, slab_rows, chip_bands)
    here, there = (blocks[:, half].reshape(-1, chip_bands) for half in range(Z_HI))
    own = jnp.concatenate([here, from_other_half(there)], axis=0)
    other = from_other_core(own)
    own_shape = (X * CORE, 2 * row_count, chip_bands)
    own, other = own.reshape(own_shape), other.reshape(own_shape)
    left = left_operators(
        partner,
        b_vectors,
        lattice_shift,
        own,
        other,
        projectors,
        jnp.transpose(support),
        proj_counts.reshape(1, -1),
        jnp.transpose(aug_matrices, (1, 2, 0)).reshape(-1, support.shape[0]),
        jnp.transpose(atom_sites),
    )
    left = left.reshape(2, left.shape[1] * left.shape[2], left.shape[3])

    near, far = (held, from_left, from_right), (far_left, far_right)
    depth, part = left.shape[1], left.shape[1] // X
    total = product(theirs_near_kernel, jnp.float32, depth - part, left, *near)
    theirs = product(
        theirs_far_kernel, jnp.bfloat16, part, left, total, *far, partner=partner
    )
    got = from_other_core(theirs)
    mine = product(mine_kernel, jnp.bfloat16, depth, left, *near, *far, partner=partner)
    final = jnp.concatenate(
        [jnp.where(core == 0, mine, got), jnp.where(core == 0, got, mine)], axis=2
    )
    return final.reshape(1, 2, 2, bands // SLABS, bands)


def solution(mesh):
    in_specs = (
        P("ka", "grid", None, None),
        P(),
        P(),
        P(),
        P(),
        P(),
        P(),
        P("ka", None),
        P("ka", None, None),
    )
    out_specs = P("ka", None, None, "grid", None)
    return jax.shard_map(body, mesh=mesh, in_specs=in_specs, out_specs=out_specs, check_vma=False)
```

```python
import functools
import math

import jax
import jax.numpy as jnp
from jax import lax
from jax.experimental import pallas as pl
from jax.experimental.pallas import tpu as pltpu
from jax.sharding import PartitionSpec as P

SIDE = 16
DEPTH = 96
TWO_PI = 2.0 * math.pi

Z_LO, Y, Z_HI, X, CORE = 4, 8, 2, 4, 2
Z = Z_LO * Z_HI
POINTS = Z_LO * Y
AXES = ("ka", "grid")
SLABS = 16
SLAB_ROWS = 32
PER_ATOM = 8
HIGHEST = lax.Precision.HIGHEST


def flat_id(x, y, z, core):
    return (((z % Z_LO) * Y + y) * Z_HI + z // Z_LO) * (X * CORE) + x * CORE + core


def route(source_of):
    pairs = []
    for x in range(X):
        for y in range(Y):
            for z in range(Z):
                for core in range(CORE):
                    sx, sy, sz, sc = source_of(x, y, z, core)
                    pairs.append(
                        (flat_id(sx % X, sy % Y, sz % Z, sc), flat_id(x, y, z, core))
                    )
    return pairs


def moved(block, source_of):
    return lax.ppermute(block, AXES, route(source_of))


def from_other_core(block):
    return moved(block, lambda x, y, z, core: (x, y, z, 1 - core))


def from_x(block, offset):
    return moved(block, lambda x, y, z, core: (x + offset, y, z, core))


def z_offset(distance, core, y):
    part = (distance // Y + 2 + (y + distance % Y) // Y) % Z_LO
    other_way = (part == 2) * core * (distance % Y != 0)
    return part - Z_LO * (part == 3) - Z_LO * other_way


class Place:
    def __init__(self, partner):
        point, member = lax.axis_index("ka"), lax.axis_index("grid")
        self.core = member & (CORE - 1)
        self.x = (member >> 1) & (X - 1)
        self.z_hi = member >> 3
        self.y = point & (Y - 1)
        self.z = self.z_hi * Z_LO + (point >> 3)
        distances = [(partner[0, v] - point) & (POINTS - 1) for v in range(2)]
        along = [d & (Y - 1) for d in distances]
        hops = [jnp.where(d == Y // 2, 2, jnp.minimum(d, Y - d)) for d in along]
        swapped = hops[0] > hops[1]
        self.swap = jnp.where(swapped, 1, 0)
        self.distances = [
            jnp.where(swapped, distances[1 - v], distances[v]) for v in range(2)
        ]

    def first_hi(self, v):
        distance = self.distances[v]
        along = distance & (Y - 1)
        part = ((distance >> 3) + 2 + ((self.y + along) >> 3)) & (Z_LO - 1)
        other_way = (part == 2) & (self.core == 1) & (along != 0)
        back = jnp.where((part == 3) | other_way, Z_LO, 0)
        return ((self.z - 2 + part - back) & (Z - 1)) >> 2


def from_other_half(block):
    return moved(block, lambda x, y, z, core: (x, y, z + Z_LO, core))


def toward_partner(lane, distance):
    def source(x, y, z, core):
        return x, (y + distance) % Y, z + z_offset(distance, core, y), core

    if all(source(0, y, 0, c) == (0, y, 0, c) for y in range(Y) for c in range(CORE)):
        return lane
    return moved(lane, source)


def both_halves(lane):
    behind = moved(lane, lambda x, y, z, core: (x, y, z - 2, core))
    ahead = moved(lane, lambda x, y, z, core: (x, y, z + 2, core))
    return behind, ahead


def dot00(left, right, precision=None):
    return lax.dot_general(
        left,
        right,
        (((0,), (0,)), ((), ())),
        precision=precision,
        preferred_element_type=jnp.float32,
    )


def left_kernel(
    partner_ref,
    b_ref,
    shift_ref,
    own_ref,
    other_ref,
    proj_ref,
    support_ref,
    counts_ref,
    aug_ref,
    sites_ref,
    out_ref,
    real_ref,
    imag_ref,
    masked_ref,
    both_ref,
):
    atoms = support_ref.shape[1]
    nproj = proj_ref.shape[1]
    rows = proj_ref.shape[0]
    width = own_ref.shape[2] // 2
    place = Place(partner_ref)
    core = place.core
    f32 = jnp.float32

    atom_of = lax.broadcasted_iota(jnp.int32, (atoms, nproj), 1) // PER_ATOM
    spread = (atom_of == lax.broadcasted_iota(jnp.int32, (atoms, nproj), 0)).astype(f32)
    reach = jnp.dot(support_ref[...].astype(f32), spread, preferred_element_type=f32)
    counts = jnp.broadcast_to(counts_ref[...].astype(f32), (8, atoms))
    counts = jnp.dot(counts, spread, preferred_element_type=f32)[0:1]
    slot_id = (lax.broadcasted_iota(jnp.int32, (1, nproj), 1) % PER_ATOM).astype(f32)
    keep = reach * (slot_id < counts - 0.5).astype(f32)
    both_ref[core] = own_ref[...]
    both_ref[1 - core] = other_ref[...]
    for s in range(SLABS):
        at = pl.ds(s * SLAB_ROWS, SLAB_ROWS)
        masked_ref[at, :] = (proj_ref[at, :].astype(f32) * keep[s : s + 1, :]).astype(
            jnp.bfloat16
        )
        slab_hi, slab_x, slab_core = s // (CORE * X), s // CORE % X, s % CORE
        slab = X * (slab_hi ^ place.z_hi) + ((place.x - slab_x) & (X - 1))
        for side in range(2):
            lanes = pl.ds(pl.multiple_of((core ^ side) * width, width), width)
            to = pl.ds(side * width, width)
            real_ref[at, to] = both_ref[slab_core, slab, pl.ds(0, SLAB_ROWS), lanes]
            imag_ref[at, to] = both_ref[slab_core, slab, pl.ds(SLAB_ROWS, SLAB_ROWS), lanes]

    masked = masked_ref[...]
    proj_real = dot00(masked, real_ref[...]).astype(jnp.bfloat16).astype(f32)
    proj_imag = dot00(masked, imag_ref[...]).astype(jnp.bfloat16).astype(f32)

    by_pair = jnp.dot(aug_ref[...], spread, precision=HIGHEST, preferred_element_type=f32)
    column = lax.broadcasted_iota(jnp.int32, (PER_ATOM, nproj), 1) % PER_ATOM
    pick = column == lax.broadcasted_iota(jnp.int32, (PER_ATOM, nproj), 0)
    by_row = [
        jnp.sum(
            jnp.where(pick, by_pair[i * PER_ATOM : (i + 1) * PER_ATOM], 0.0),
            axis=0,
            keepdims=True,
        )
        for i in range(PER_ATOM)
    ]
    tiled = jnp.concatenate(by_row * atoms, axis=0)
    same_atom = (
        lax.broadcasted_iota(jnp.int32, (nproj, nproj), 0) // PER_ATOM
        == lax.broadcasted_iota(jnp.int32, (nproj, nproj), 1) // PER_ATOM
    )
    aug = jnp.where(same_atom, tiled, 0.0)
    aug_real = dot00(aug, proj_real, HIGHEST)
    aug_imag = dot00(aug, proj_imag, HIGHEST)

    sites = jnp.dot(sites_ref[...], spread, precision=HIGHEST, preferred_element_type=f32)
    chunks = rows // 128
    lanes = lax.broadcasted_iota(jnp.int32, (8, 128), 1)
    block = lax.broadcasted_iota(jnp.int32, (8, 128), 0)
    row_ids = block * 128 + lanes
    along_a = (row_ids % SIDE).astype(f32) / SIDE
    along_b = (row_ids // SIDE % SIDE).astype(f32) / SIDE
    along_c = (row_ids // (SIDE * SIDE)).astype(f32) / DEPTH

    for v in range(2):
        vector = v ^ place.swap
        first_hi = place.first_hi(v)
        q = [
            b_ref[vector, axis] + shift_ref[0, vector, axis].astype(f32)
            for axis in range(3)
        ]
        theta = TWO_PI * (q[0] * along_a + q[1] * along_b + q[2] * along_c)
        phi = TWO_PI * (q[0] * sites[0:1] + q[1] * sites[1:2] + q[2] * sites[2:3])
        angle = theta
        for part in range(nproj // 128):
            piece = phi[0:1, part * 128 : (part + 1) * 128]
            angle = jnp.where(block == chunks + part, piece, angle)
        cosine = jnp.transpose(jnp.cos(angle))
        sine = jnp.transpose(jnp.sin(angle))
        weights = []
        for part in range(nproj // 128):
            at = slice(part * 128, (part + 1) * 128)
            cos_p = cosine[:, chunks + part : chunks + part + 1]
            sin_p = sine[:, chunks + part : chunks + part + 1]
            weights.append(
                (
                    cos_p * aug_real[at] - sin_p * aug_imag[at],
                    cos_p * aug_imag[at] + sin_p * aug_real[at],
                )
            )
        weight_real = jnp.concatenate([w[0] for w in weights], axis=0)
        weight_imag = jnp.concatenate([w[1] for w in weights], axis=0)

        def spread_rows(weight):
            high = weight.astype(jnp.bfloat16)
            low = (weight - high.astype(f32)).astype(jnp.bfloat16)
            return jnp.dot(masked, high, preferred_element_type=f32) + jnp.dot(
                masked, low, preferred_element_type=f32
            )

        added_real = spread_rows(weight_real)
        added_imag = spread_rows(weight_imag)
        per_chunk = 128 // SLAB_ROWS
        for s in range(SLABS):
            chunk, inside = s // per_chunk, s % per_chunk * SLAB_ROWS
            at = slice(s * SLAB_ROWS, (s + 1) * SLAB_ROWS)
            cos_r = cosine[inside : inside + SLAB_ROWS, chunk : chunk + 1]
            sin_r = sine[inside : inside + SLAB_ROWS, chunk : chunk + 1]
            wave_real = real_ref[at, :].astype(f32)
            wave_imag = imag_ref[at, :].astype(f32)
            left_real = cos_r * wave_real - sin_r * wave_imag + added_real[at]
            left_imag = cos_r * wave_imag + sin_r * wave_real + added_imag[at]
            left_real = left_real.astype(jnp.bfloat16)
            left_imag = left_imag.astype(jnp.bfloat16)
            slab_hi, slab_x, slab_core = s // (CORE * X), s // CORE % X, s % CORE
            step = (slab_x - place.x) & (X - 1)
            piece = jnp.where(step == 3, 1, jnp.where(step == 0, 0, step + 1))
            slot = piece * 4 + (slab_hi ^ first_hi) * 2 + (slab_core ^ core)
            top, low = pl.ds(0, SLAB_ROWS), pl.ds(SLAB_ROWS, SLAB_ROWS)
            for side in range(2):
                real_half = left_real[:, side * width : (side + 1) * width]
                imag_half = left_imag[:, side * width : (side + 1) * width]
                base = side * 2 * width
                out_ref[v, slot, top, base : base + width] = real_half
                out_ref[v, slot, low, base : base + width] = imag_half
                out_ref[v, slot, top, base + width : base + 2 * width] = -imag_half
                out_ref[v, slot, low, base + width : base + 2 * width] = real_half


def left_operators(partner, b_vectors, shift, own, other, projectors, support, counts, aug, sites):
    rows, nproj = projectors.shape
    width = own.shape[2] // 2
    smem = pl.BlockSpec(memory_space=pltpu.SMEM)
    vmem = pl.BlockSpec(memory_space=pltpu.VMEM)
    return pl.pallas_call(
        left_kernel,
        out_shape=jax.ShapeDtypeStruct((2, SLABS, 2 * SLAB_ROWS, 4 * width), jnp.bfloat16),
        in_specs=[smem] * 3 + [vmem] * 7,
        out_specs=vmem,
        scratch_shapes=[
            pltpu.VMEM((rows, 2 * width), jnp.bfloat16),
            pltpu.VMEM((rows, 2 * width), jnp.bfloat16),
            pltpu.VMEM((rows, nproj), jnp.bfloat16),
            pltpu.VMEM((2,) + own.shape, jnp.bfloat16),
        ],
        compiler_params=pltpu.CompilerParams(vmem_limit_bytes=28 * 1024 * 1024),
        cost_estimate=pl.CostEstimate(
            flops=2_000_000_000, bytes_accessed=4 * 1024 * 1024, transcendentals=4096
        ),
        name="left_operators",
    )(partner, b_vectors, shift, own, other, projectors, support, counts, aug, sites)


def near_rows(v, held, from_left, from_right):
    rows = held.shape[0] // 2
    return [ref[v * rows : (v + 1) * rows, :] for ref in (held, from_left, from_right)]


def far_rows(v, far_left, far_right):
    rows = far_left.shape[0] // 2
    return [ref[v * rows : (v + 1) * rows, :] for ref in (far_left, far_right)]


def near_kernel(left_ref, held, from_left, from_right, total_ref):
    for v in range(2):
        right = jnp.concatenate(near_rows(v, held, from_left, from_right), axis=0)
        total_ref[v] = dot00(left_ref[v, : right.shape[0], :], right)


def far_kernel(side, partner_ref, left_ref, total_ref, far_left, far_right, out_ref):
    swap = Place(partner_ref).swap
    half = left_ref.shape[2] // 2
    at = slice(side * half, (side + 1) * half)
    for v in range(2):
        right = jnp.concatenate(far_rows(v, far_left, far_right), axis=0)
        last = dot00(left_ref[v, -right.shape[0] :, at], right)
        out_ref[v ^ swap] = (total_ref[v, at] + last).astype(jnp.bfloat16)


def product(kernel, dtype, depth, sides, *operands, partner=None):
    left, columns = operands[0], operands[-1].shape[1]
    half = sides * (left.shape[2] // 2)
    smem = pl.BlockSpec(memory_space=pltpu.SMEM)
    vmem = pl.BlockSpec(memory_space=pltpu.VMEM)
    first = () if partner is None else (partner,)
    return pl.pallas_call(
        kernel,
        out_shape=jax.ShapeDtypeStruct((2, half, columns), dtype),
        in_specs=[smem] * len(first) + [vmem] * len(operands),
        out_specs=vmem,
        compiler_params=pltpu.CompilerParams(vmem_limit_bytes=28 * 1024 * 1024),
        cost_estimate=pl.CostEstimate(
            flops=4 * depth * half * columns,
            bytes_accessed=1024 * 1024,
            transcendentals=0,
        ),
        name="product",
    )(*first, *operands)


def body(
    wavefunctions,
    projectors,
    support,
    proj_counts,
    aug_matrices,
    atom_sites,
    b_vectors,
    partner,
    lattice_shift,
):
    waves = wavefunctions[0]
    row_count, _, bands = waves.shape
    half_bands = bands // CORE
    place = Place(partner)
    core, x, z_hi, distances = place.core, place.x, place.z_hi, place.distances

    slab = jnp.transpose(waves, (1, 0, 2)).reshape(2 * row_count, bands)
    low, high = slab[:, :half_bands], slab[:, half_bands:]
    kept = jnp.where(core == 0, low, high)
    given = jnp.where(core == 0, high, low)
    lane = jnp.concatenate([kept, from_other_core(given)], axis=0)
    half_rows = lane.shape[0]

    chip_bands = half_bands // X

    def bands_of(offset):
        blocks = [
            lax.dynamic_slice_in_dim(
                slab, (half * X + ((x + offset) & (X - 1))) * chip_bands, chip_bands, axis=1
            )
            for half in (z_hi, 1 - z_hi)
        ]
        return jnp.concatenate(blocks, axis=0)

    def first_stage(distance, lane):
        onward = jnp.concatenate([bands_of(1), bands_of(2)], axis=0)
        return (
            toward_partner(lane, distance),
            from_x(onward, -1),
            from_x(bands_of(-1), 1),
        )

    def second_stage(distance, lane, moved_first, onward):
        held_first = both_halves(moved_first)
        return (
            toward_partner(lane, distance),
            held_first,
            from_x(onward, -1),
        )

    moved_first, one_back, one_on = lax.switch(
        distances[0],
        [functools.partial(first_stage, d) for d in range(POINTS)],
        lane,
    )
    moved_second, held_first, two_back = lax.switch(
        distances[1],
        [functools.partial(second_stage, d) for d in range(POINTS)],
        lane,
        moved_first,
        one_back,
    )
    held_second = both_halves(moved_second)
    held = jnp.concatenate([*held_first, *held_second], axis=0)
    from_left, from_right = from_x(held, -1), from_x(held, 1)

    def of_both(block, half):
        rows = [block[i * half_rows : (i + 1) * half_rows] for i in (half, 2 + half)]
        return jnp.concatenate(rows, axis=0)

    far_left = from_x(of_both(from_left, 0), -1)
    far_right = from_x(of_both(from_right, 1), 1)
    along_x = (bands_of(0), one_back[:half_rows], two_back[half_rows:], one_on)
    slab_rows = 2 * row_count
    blocks = jnp.concatenate(along_x, axis=0).reshape(X, Z_HI, slab_rows, chip_bands)
    here, there = (blocks[:, half].reshape(-1, chip_bands) for half in range(Z_HI))
    own = jnp.concatenate([here, from_other_half(there)], axis=0)
    other = from_other_core(own)
    own_shape = (X * CORE, 2 * row_count, chip_bands)
    own, other = own.reshape(own_shape), other.reshape(own_shape)
    left = left_operators(
        partner,
        b_vectors,
        lattice_shift,
        own,
        other,
        projectors,
        jnp.transpose(support),
        proj_counts.reshape(1, -1),
        jnp.transpose(aug_matrices, (1, 2, 0)).reshape(-1, support.shape[0]),
        jnp.transpose(atom_sites),
    )
    left = left.reshape(2, left.shape[1] * left.shape[2], left.shape[3])

    near, far = (held, from_left, from_right), (far_left, far_right)
    depth, part = left.shape[1], left.shape[1] // X
    total = product(near_kernel, jnp.float32, depth - part, 2, left, *near)

    def finished(side):
        kernel = functools.partial(far_kernel, side)
        return product(kernel, jnp.bfloat16, part, 1, left, total, *far, partner=partner)

    theirs = finished(1)
    got = from_other_core(theirs)
    mine = finished(0)
    final = jnp.concatenate(
        [jnp.where(core == 0, mine, got), jnp.where(core == 0, got, mine)], axis=2
    )
    return final.reshape(1, 2, 2, bands // SLABS, bands)


def solution(mesh):
    in_specs = (
        P("ka", "grid", None, None),
        P(),
        P(),
        P(),
        P(),
        P(),
        P(),
        P("ka", None),
        P("ka", None, None),
    )
    out_specs = P("ka", None, None, "grid", None)
    return jax.shard_map(body, mesh=mesh, in_specs=in_specs, out_specs=out_specs, check_vma=False)
```
